32 devices in a mesh: dp: 8 (over z, y), ctx: 4 (over x, core).
Axes of the slice: x: 2, y: 2, z: 4, core: 2. Of those that a mesh axis runs over, the one named last changes fastest.
Arguments:
- tokens: bfloat16 [4096, 1024], P(('dp', 'ctx')), parts along dimension 0, may hold values from -6 to 6
- queries: bfloat16 [4096, 1024], P(('dp', 'ctx')), parts along dimension 0, may hold values from -128 to 128
- key_weight: bfloat16 [1024, 1024], replicated, may hold values from -0.1875 to 0.1875
- value_weight: bfloat16 [1024, 1024], replicated, may hold values from -0.1875 to 0.1875
- lengths: int32 [48], P('dp'), parts along dimension 0, may hold values from 1 to 256, 512 in all
- dest_slot: int32 [128], P('dp'), parts along dimension 0, may hold values from 0 to 15, as said below
- block_mask: int32 [128, 16], P('dp'), parts along dimension 0, may hold values 0 or 1
Outputs:
- attended: bfloat16 [4096, 1024], P(('dp', 'ctx')), parts along dimension 0
The draws below stay inside these ranges and needn't reach their ends.
There are 8 independent parts, one for each index of `dp`. The reference program is written for one: setup_inputs(seed, part) draws one part's arguments, and reference() takes and returns one part's arrays. A program takes and returns all parts, laid end to end along the dimension named above; an argument that names none is the same for every part. Nothing has to cross between parts.
Inputs may be any that keep to these rules, and one draw needn't show every extreme that they name: dest_slot is a permutation of the 16 slots; slot r lies on device r // 4. The 4 blocks that start on one device go in two pairs to two different devices, so every device receives exactly 2 blocks from each of two devices.
All inputs are finite; a program needn't handle non-finite values.
Results may differ from the reference program's by a relative error of at most 0.012.
The reference program's roundings to bfloat16 on the way (of `key_rows`, `value_rows` and `rounded_weights`) count: a program that leaves them out, or rounds other values in their place, can miss the bound.
Values may be sent and summed in bfloat16 or wider, within the bound.
A program may use at most 64 MiB of HBM per device.

```python
import math
import jax
import jax.numpy as jnp
import numpy as np
from jax import lax

D = 1024
HEADS = 8
HD = 128
TOK_DEV = 128
BLOCKS_DEV = 4
CLIPS = 6
SEQ = 512
NBLK = 16
CLIP_MOST = 256


def draw_queries(key, part):
    first_key = jax.random.fold_in(key, 0)
    inner_width = HEADS * HD
    result = jnp.clip(jax.random.normal(first_key, (SEQ, inner_width), jnp.float32), -4.0, 4.0)
    return result.astype(jnp.bfloat16)


def shuffled(sub_key):
    return jax.random.permutation(sub_key, BLOCKS_DEV).astype(jnp.int32)


def draw_dest_slot(key, part):
    keys_all = jax.random.split(key, 4)
    devices = NBLK // BLOCKS_DEV
    half_count = BLOCKS_DEV // 2
    order_dev = jax.random.permutation(keys_all[0], devices).astype(jnp.int32)
    offset = jax.random.randint(keys_all[1], (), 1, devices).astype(jnp.int32)
    sources = jnp.arange(devices, dtype=jnp.int32)
    first_dest = order_dev
    second_dest = order_dev[(sources + offset) % devices]
    local_order = jax.vmap(shuffled)(jax.random.split(keys_all[2], devices))
    slot_order = jax.vmap(shuffled)(jax.random.split(keys_all[3], devices))
    first_slots = slot_order[first_dest][:, :half_count]
    second_slots = slot_order[second_dest][:, half_count:]
    dest_device = jnp.concatenate([jnp.repeat(first_dest[:, None], half_count, axis=1), jnp.repeat(second_dest[:, None], half_count, axis=1)], axis=1)
    dest_local = jnp.concatenate([first_slots, second_slots], axis=1)
    target = dest_device * BLOCKS_DEV + dest_local
    block_index = sources[:, None] * BLOCKS_DEV + local_order
    return jnp.zeros((NBLK,), jnp.int32).at[block_index.reshape(-1)].set(target.reshape(-1))


def place_ends(array, stream_key, low, largest):
    dims = array.shape
    place = [jax.random.randint(jax.random.fold_in(stream_key, axis), (), 0, dims[axis]) for axis in range(len(dims))]
    array = array.at[tuple(place)].set(low)
    longest = dims.index(max(dims))
    place[longest] = (place[longest] + 1) % dims[longest]
    return array.at[tuple(place)].set(largest)


def block_levels(key, shape, cuts, smallest, largest):
    factor_of = 1.0
    for dim, shards_of in cuts:
        steps = jax.random.uniform(jax.random.fold_in(jax.random.fold_in(key, 6), dim), (shards_of,), jnp.float32, smallest / len(cuts), largest / len(cuts))
        factor_of = factor_of * jnp.repeat(jnp.exp(steps), shape[dim] // shards_of).reshape((-1,) + (1,) * (len(shape) - 1 - dim))
    return factor_of


def profile(count, total, reach, slope):
    loads = [(1 << 20) // math.isqrt(grade ** slope) + 1 for grade in range(2, count + 1)]
    spare, given = total - reach - (count - 1), [1] * (count - 1)
    while spare > 0:
        movable = [i for i in range(count - 1) if given[i] < reach]
        whole, remaining = sum([loads[i] for i in movable]), spare
        for i in movable:
            extra = min(reach - given[i], max(1, remaining * loads[i] // whole), spare)
            given[i] = given[i] + extra
            spare = spare - extra
    return np.array([reach] + given)


def uneven(stream_key, amount, total, reach, slope):
    if amount == 2:
        one = jax.random.randint(stream_key, (), max(1, total - reach), min(reach, total - 1) + 1)
        return jnp.stack([one, total - one])
    tallies = jnp.asarray(profile(amount, total, reach, slope), jnp.int32)
    pairs = (amount - 1) // 2
    donor, receiver = tallies[1:1 + 2 * pairs:2], tallies[2:2 + 2 * pairs:2]
    slack = jnp.minimum(donor - 1, reach - receiver)
    moved = jax.random.randint(jax.random.fold_in(stream_key, 1), (pairs,), 0, 1 << 20) % (slack + 1)
    tallies = tallies.at[1:1 + 2 * pairs:2].set(donor - moved).at[2:2 + 2 * pairs:2].set(receiver + moved)
    return tallies[jax.random.permutation(jax.random.fold_in(stream_key, 2), amount)]


def normal_values(rng, dims, scale, most, shards=(), held_as=jnp.bfloat16):
    values = scale * jax.random.normal(rng, dims, jnp.float32)
    if shards:
        values = values * block_levels(rng, dims, shards, -0.22, 0.18)
    return jnp.clip(values, -most, most).astype(held_as)


def setup_inputs(seed: int = 0, part: int = 0) -> dict:
    arg_keys = jax.random.split(jax.random.key(seed), 8)
    part_keys = jax.random.split(jax.random.fold_in(arg_keys[7], part), 8)
    return {
        "tokens": normal_values(part_keys[0], (SEQ, D), 1.0, 6.0, ((0, 4),)),
        "queries": draw_queries(jax.random.fold_in(jax.random.fold_in(arg_keys[7], part), 71), part),
        "key_weight": normal_values(arg_keys[2], (D, HEADS * HD), D ** -0.5, 0.1875),
        "value_weight": normal_values(arg_keys[3], (D, HEADS * HD), D ** -0.5, 0.1875),
        "lengths": uneven(part_keys[4], CLIPS, SEQ, CLIP_MOST, 2).astype(jnp.int32),
        "dest_slot": draw_dest_slot(jax.random.fold_in(jax.random.fold_in(arg_keys[7], part), 71), part),
        "block_mask": place_ends((jax.random.randint(part_keys[6], (NBLK, NBLK), 0, 2) < 1).astype(jnp.int32), jax.random.fold_in(part_keys[6], 1), 0, 1),
    }


def clip_index(position, lengths):
    bounds = jnp.cumsum(lengths)
    return jnp.sum((position[:, None] >= bounds[None, :]).astype(jnp.int32), axis=1)


def reference(tokens, queries, key_weight, value_weight, lengths, dest_slot, block_mask):
    seq_len = tokens.shape[0]
    block_count = dest_slot.shape[0]
    block_rows = seq_len // block_count
    inner_width = HEADS * HD
    key_rows = jnp.dot(tokens, key_weight, preferred_element_type=jnp.float32).astype(jnp.bfloat16)
    value_rows = jnp.dot(tokens, value_weight, preferred_element_type=jnp.float32).astype(jnp.bfloat16)
    positions = jnp.arange(seq_len, dtype=jnp.int32)
    clip_ids = clip_index(positions, lengths)
    block_ids = positions // block_rows
    keys_three = key_rows.astype(jnp.float32).reshape(seq_len, HEADS, HD)
    values_three = value_rows.astype(jnp.float32).reshape(seq_len, HEADS, HD)
    score_scale = 1.0 / (HD ** 0.5)

    def one_block(start):
        query_block = lax.dynamic_slice_in_dim(queries, start, TOK_DEV, 0).astype(jnp.float32).reshape(TOK_DEV, HEADS, HD)
        scores = jnp.einsum("qhd,khd->hqk", query_block, keys_three) * score_scale
        query_pos = start + jnp.arange(TOK_DEV, dtype=jnp.int32)
        query_clip = clip_index(query_pos, lengths)
        query_block_id = query_pos // block_rows
        linked = block_mask[query_block_id][:, block_ids] == 1
        allowed = (query_clip[:, None] == clip_ids[None, :]) & ((query_block_id[:, None] == block_ids[None, :]) | linked)
        masked = jnp.where(allowed[None], scores, jnp.float32(-1e30))
        row_max = jnp.max(masked, axis=-1)
        weights_exp = jnp.where(allowed[None], jnp.exp(masked - row_max[..., None]), jnp.float32(0.0))
        total = jnp.sum(weights_exp, axis=-1)
        rounded_weights = lax.optimization_barrier(weights_exp.astype(jnp.bfloat16)).astype(jnp.float32)
        mixed = jnp.einsum("hqk,khd->qhd", rounded_weights, values_three) / total.T[:, :, None]
        return mixed.reshape(TOK_DEV, inner_width).astype(jnp.bfloat16)

    starts = jnp.arange(seq_len // TOK_DEV, dtype=jnp.int32) * TOK_DEV
    mixed_all = lax.map(one_block, starts).reshape(block_count, block_rows, inner_width)
    source_block = jnp.zeros((block_count,), jnp.int32).at[dest_slot].set(jnp.arange(block_count, dtype=jnp.int32))
    return mixed_all[source_block].reshape(seq_len, inner_width)
```

```python
import jax
import jax.numpy as jnp
from jax import lax
from jax.experimental import pallas as pl
from jax.experimental.pallas import tpu as pltpu
from jax.sharding import PartitionSpec as P

HEADS = 8
HD = 128
BLOCKS_DEV = 4


def clip_index(position, lengths):
    order = jnp.arange(lengths.shape[0], dtype=jnp.int32)
    bounds = jnp.sum(jnp.where(order[None, :] <= order[:, None], lengths[None, :], 0), axis=1)
    return jnp.sum((position[:, None] >= bounds[None, :]).astype(jnp.int32), axis=1)


def collect_rows(wanted, carry, pieces):
    count = pieces[0].shape[0]
    inside = (wanted >= 0) & (wanted < count)
    position = jnp.clip(wanted, 0, count - 1)
    return tuple(
        (
            jnp.where(inside[:, None], jnp.take(piece, position, axis=0), kept)
            for piece, kept in zip(pieces, carry)
        )
    )


def on_device(tokens, queries, key_weight, value_weight, lengths, dest_slot, block_mask):
    device_id = lax.axis_index("ctx")
    row_count = tokens.shape[0]
    inner_width = queries.shape[1]
    block_rows = row_count // BLOCKS_DEV
    block_count = dest_slot.shape[0]
    block_ids = jnp.arange(block_count, dtype=jnp.int32)
    source_block = jnp.zeros((block_count,), jnp.int32).at[dest_slot].set(block_ids)
    my_slots = device_id * BLOCKS_DEV + jnp.arange(BLOCKS_DEV, dtype=jnp.int32)
    mine = source_block[my_slots]
    offsets = jnp.arange(block_rows, dtype=jnp.int32)
    wanted = (mine[:, None] * block_rows + offsets[None, :]).reshape(row_count)
    start_rows = (jnp.zeros_like(tokens), jnp.zeros_like(queries))
    moved_tokens, moved_queries = collect_rows(
        wanted,
        start_rows,
        (
            lax.all_gather(tokens, "ctx", axis=0, tiled=True),
            lax.all_gather(queries, "ctx", axis=0, tiled=True),
        ),
    )
    key_rows = jnp.dot(moved_tokens, key_weight, preferred_element_type=jnp.float32).astype(
        jnp.bfloat16
    )
    value_rows = jnp.dot(moved_tokens, value_weight, preferred_element_type=jnp.float32).astype(
        jnp.bfloat16
    )
    query_clip = clip_index(wanted, lengths)
    query_block_id = wanted // block_rows
    onehot_query = (query_block_id[:, None] == block_ids[None, :]).astype(jnp.float32)
    mask_rows = jnp.dot(onehot_query, block_mask.astype(jnp.float32))
    query_three = moved_queries.reshape(row_count, HEADS, HD)
    score_scale = 1.0 / HD**0.5
    key_piece = lax.all_gather(key_rows, "ctx", axis=0, tiled=True)
    value_piece = lax.all_gather(value_rows, "ctx", axis=0, tiled=True)
    count = key_piece.shape[0]
    key_slot = jnp.arange(count, dtype=jnp.int32)
    key_block = source_block[key_slot // block_rows]
    key_pos = key_block * block_rows + key_slot % block_rows
    key_clip = clip_index(key_pos, lengths)
    onehot_key = (block_ids[:, None] == key_block[None, :]).astype(jnp.float32)
    linked = jnp.dot(mask_rows, onehot_key) > 0.5
    allowed = (query_clip[:, None] == key_clip[None, :]) & (
        (query_block_id[:, None] == key_block[None, :]) | linked
    )
    scores = (
        jnp.einsum(
            "qhd,khd->hqk",
            query_three,
            key_piece.reshape(count, HEADS, HD),
            preferred_element_type=jnp.float32,
        )
        * score_scale
    )
    run_max = jnp.full((HEADS, row_count), -1e30, jnp.float32)
    run_acc = jnp.zeros((row_count, HEADS, HD), jnp.float32)
    masked = jnp.where(allowed[None], scores, jnp.float32(-1e30))
    new_max = jnp.maximum(run_max, jnp.max(masked, axis=-1))
    rescale = jnp.exp(run_max - new_max)
    weights_exp = jnp.where(allowed[None], jnp.exp(masked - new_max[..., None]), jnp.float32(0.0))
    new_total = jnp.sum(weights_exp, axis=-1)
    partial_value = jnp.einsum(
        "hqk,khd->qhd",
        weights_exp.astype(jnp.bfloat16),
        value_piece.reshape(count, HEADS, HD),
        preferred_element_type=jnp.float32,
    )
    new_acc = run_acc * rescale.T[:, :, None] + partial_value
    finished = (
        (new_acc / new_total.T[:, :, None]).reshape(row_count, inner_width).astype(jnp.bfloat16)
    )
    return finished


TOK_CHUNKS = 4
Q_CHUNKS = 2
LOG2E = 1.4426950408889634


def fused_kernel(
    dest,
    lengths,
    mask_ref,
    tok_hbm,
    q_hbm,
    kw_hbm,
    vw_hbm,
    out_ref,
    tok,
    q_own,
    q_send,
    q_all,
    kw,
    vw,
    keys,
    values,
    linked,
    result,
    load_sem,
    tok_send,
    tok_recv,
    relay_send,
    relay_recv,
    near_send,
    near_recv,
    q_ssem,
    q_rsem,
):
    rows, width = tok_hbm.shape
    block_rows = rows // BLOCKS_DEV
    seq = 4 * rows
    blocks = 4 * BLOCKS_DEV
    heads = width // HD
    me = lax.axis_index("ctx")
    near = me + 1 - 2 * (me % 2)
    far = me + 2 - 4 * (me // 2)
    cross = 3 - me
    peers = (me, near, far, cross)

    loads = [
        pltpu.make_async_copy(tok_hbm, tok.at[0], load_sem.at[0]),
        pltpu.make_async_copy(q_hbm, q_own, load_sem.at[1]),
        pltpu.make_async_copy(kw_hbm, kw, load_sem.at[2]),
        pltpu.make_async_copy(vw_hbm, vw, load_sem.at[3]),
    ]
    for load in loads:
        load.start()

    barrier = pltpu.get_barrier_semaphore()
    for peer in peers[1:]:
        pl.semaphore_signal(
            barrier, inc=1, device_id={"ctx": peer}, device_id_type=pl.DeviceIdType.MESH
        )
    pl.semaphore_wait(barrier, 3)

    def send(source, target, send_sem, recv_sem, peer):
        return pltpu.make_async_remote_copy(
            src_ref=source,
            dst_ref=target,
            send_sem=send_sem,
            recv_sem=recv_sem,
            device_id={"ctx": peer},
            device_id_type=pl.DeviceIdType.MESH,
        )

    step = rows // TOK_CHUNKS
    far_copies = []
    relay_copies = []
    for c in range(TOK_CHUNKS):
        part = pl.ds(c * step, step)
        far_copies.append(
            send(tok_hbm.at[part], tok.at[2, part], tok_send.at[c], tok_recv.at[c], far)
        )
        relay_copies.append(
            send(tok.at[2, part], tok.at[3, part], relay_send.at[c], relay_recv.at[c], near)
        )
        far_copies[c].start()
    near_copy = send(tok_hbm, tok.at[1], near_send.at[0], near_recv.at[0], near)
    near_copy.start()

    def two_blocks(source, to):
        count = jnp.int32(0)
        first = jnp.int32(0)
        second = jnp.int32(0)
        for b in range(BLOCKS_DEV):
            hit = dest[source * BLOCKS_DEV + b] // BLOCKS_DEV == to
            first = jnp.where(hit & (count == 0), b, first)
            second = jnp.where(hit & (count == 1), b, second)
            count = count + hit.astype(jnp.int32)
        return first, second

    loads[1].wait()
    qw = width // Q_CHUNKS
    q_copies = {}
    pair = 2 * block_rows

    def pick(shape, pieces, wanted):
        row = lax.broadcasted_iota(jnp.int32, (block_rows, shape), 0)
        column = lax.broadcasted_iota(jnp.int32, (block_rows, shape), 1)
        return jnp.concatenate(
            [jnp.where(row + wanted[p] * block_rows == column, 1.0, 0.0) for p in range(pieces)],
            axis=0,
        ).astype(jnp.bfloat16)

    wanted = []
    for r in range(4):
        wanted.extend(two_blocks(me, peers[r]))
    chosen = pick(rows, 8, wanted)
    for c in range(Q_CHUNKS):
        packed = jnp.dot(
            chosen, q_own[:, c * qw : (c + 1) * qw], preferred_element_type=jnp.float32
        ).astype(jnp.bfloat16)
        q_all[c, 0] = packed[:pair]
        q_send[c] = packed[pair:].reshape(3, pair, qw)
        for r in (1, 3, 2):
            q_copies[c, r] = send(
                q_send.at[c, r - 1],
                q_all.at[c, r],
                q_ssem.at[c, r - 1],
                q_rsem.at[c, r - 1],
                peers[r],
            )
            q_copies[c, r].start()

    bounds = []
    running = jnp.int32(0)
    for c in range(lengths.shape[0]):
        running = running + lengths[c]
        bounds.append(running)

    def clip_of(position):
        total = jnp.zeros_like(position)
        for bound in bounds:
            total = total + jnp.where(position >= bound, 1, 0)
        return total

    col = lax.broadcasted_iota(jnp.int32, (1, seq), 1)
    slot = col // rows
    owner = jnp.where(
        slot == 0, me, jnp.where(slot == 1, near, jnp.where(slot == 2, far, cross))
    )
    key_pos = owner * rows + col % rows
    key_clip = clip_of(key_pos)
    key_block = key_pos // block_rows
    bi = lax.broadcasted_iota(jnp.int32, (blocks, blocks), 0)
    bj = lax.broadcasted_iota(jnp.int32, (blocks, blocks), 1)
    link = jnp.where((bi == bj) | (mask_ref[...] == 1), 1.0, 0.0).astype(jnp.bfloat16)
    spread = jnp.where(
        lax.broadcasted_iota(jnp.int32, (blocks, seq), 0) == key_block, 1.0, 0.0
    ).astype(jnp.bfloat16)
    linked[...] = jnp.dot(link, spread, preferred_element_type=jnp.float32).astype(jnp.bfloat16)

    def blocked_for(first):
        of_block = []
        clips = []
        for r in (first, first + 1):
            for place in two_blocks(peers[r], me):
                block = peers[r] * BLOCKS_DEV + place
                ids = lax.broadcasted_iota(jnp.int32, (block_rows, blocks), 1)
                of_block.append(jnp.where(ids == block, 1.0, 0.0))
                clips.append(
                    clip_of(
                        block * block_rows
                        + lax.broadcasted_iota(jnp.int32, (block_rows, 1), 0)
                    )
                )
        seen = jnp.dot(
            jnp.concatenate(of_block, axis=0).astype(jnp.bfloat16),
            linked[...],
            preferred_element_type=jnp.float32,
        )
        return (seen < 0.5) | (jnp.concatenate(clips, axis=0) != key_clip)

    def project(first, part, parts):
        cw = width // parts
        x = tok[first : first + 2].reshape(2 * rows, width)
        at = slice(first * rows, (first + 2) * rows)
        cols = slice(part * cw, (part + 1) * cw)
        for w, kept in ((kw, keys), (vw, values)):
            kept[at, cols] = jnp.dot(
                x, w[:, cols], preferred_element_type=jnp.float32
            ).astype(jnp.bfloat16)

    def attend(first, blocked, chunk):
        for h in range(heads // Q_CHUNKS):
            q = q_all[chunk, first : first + 2, :, h * HD : (h + 1) * HD].reshape(
                4 * block_rows, HD
            )
            at = chunk * qw + h * HD
            s = lax.dot_general(
                q, keys[:, at : at + HD], (((1,), (1,)), ((), ())),
                preferred_element_type=jnp.float32,
            )
            s = jnp.where(blocked, -jnp.inf, s)
            top = jnp.max(s, axis=1, keepdims=True)
            e = jnp.exp2((s - top) * (LOG2E / HD**0.5))
            total = jnp.sum(e, axis=1, keepdims=True)
            mixed = jnp.dot(
                e.astype(jnp.bfloat16), values[:, at : at + HD],
                preferred_element_type=jnp.float32,
            )
            result[first * 2 * block_rows : (first + 2) * 2 * block_rows, at : at + HD] = (
                mixed / total
            ).astype(jnp.bfloat16)

    near_blocked = blocked_for(0)
    far_blocked = blocked_for(2)

    loads[0].wait()
    loads[2].wait()
    loads[3].wait()
    near_copy.wait_recv()
    for c in range(TOK_CHUNKS):
        project(0, c, TOK_CHUNKS)
        far_copies[c].wait_recv()
        relay_copies[c].start()
    for c in range(TOK_CHUNKS):
        relay_copies[c].wait_recv()
    for c in range(TOK_CHUNKS):
        project(2, c, TOK_CHUNKS)
    for c in range(Q_CHUNKS):
        q_copies[c, 1].wait_recv()
        attend(0, near_blocked, c)
    for c in range(Q_CHUNKS):
        q_copies[c, 2].wait_recv()
        q_copies[c, 3].wait_recv()
        attend(2, far_blocked, c)

    wanted = []
    for t in range(BLOCKS_DEV):
        place = jnp.int32(0)
        for r in range(4):
            rank = jnp.int32(0)
            for b in range(BLOCKS_DEV):
                target = dest[peers[r] * BLOCKS_DEV + b]
                hit = target == me * BLOCKS_DEV + t
                place = jnp.where(hit, 2 * r + rank, place)
                rank = rank + (target // BLOCKS_DEV == me).astype(jnp.int32)
        wanted.append(place)
    chosen = pick(2 * rows, BLOCKS_DEV, wanted)
    out_ref[...] = jnp.dot(chosen, result[...], preferred_element_type=jnp.float32).astype(
        jnp.bfloat16
    )

    near_copy.wait_send()
    for c in range(TOK_CHUNKS):
        far_copies[c].wait_send()
        relay_copies[c].wait_send()
    for c in q_copies.values():
        c.wait_send()


def fused(tokens, queries, key_weight, value_weight, lengths, dest_slot, block_mask):
    rows, width = tokens.shape
    seq = 4 * rows
    pair = rows // 2
    bf = jnp.bfloat16
    dma = pltpu.SemaphoreType.DMA
    qw = width // Q_CHUNKS
    smem = pl.BlockSpec(memory_space=pltpu.SMEM)
    vmem = pl.BlockSpec(memory_space=pltpu.VMEM)
    hbm = pl.BlockSpec(memory_space=pl.ANY)
    return pl.pallas_call(
        fused_kernel,
        out_shape=jax.ShapeDtypeStruct((rows, width), bf),
        in_specs=[smem, smem, vmem, hbm, hbm, hbm, hbm],
        out_specs=vmem,
        scratch_shapes=[
            pltpu.VMEM((4, rows, width), bf),
            pltpu.VMEM((rows, width), bf),
            pltpu.VMEM((Q_CHUNKS, 3, pair, qw), bf),
            pltpu.VMEM((Q_CHUNKS, 4, pair, qw), bf),
            pltpu.VMEM(key_weight.shape, bf),
            pltpu.VMEM(value_weight.shape, bf),
            pltpu.VMEM((seq, width), bf),
            pltpu.VMEM((seq, width), bf),
            pltpu.VMEM((4 * BLOCKS_DEV, seq), bf),
            pltpu.VMEM((2 * rows, width), bf),
            dma((4,)),
            dma((TOK_CHUNKS,)),
            dma((TOK_CHUNKS,)),
            dma((TOK_CHUNKS,)),
            dma((TOK_CHUNKS,)),
            dma((1,)),
            dma((1,)),
            dma((Q_CHUNKS, 3)),
            dma((Q_CHUNKS, 3)),
        ],
        compiler_params=pltpu.CompilerParams(
            collective_id=0, has_side_effects=True, vmem_limit_bytes=40 * 2**20
        ),
        cost_estimate=pl.CostEstimate(
            flops=2800000000, bytes_accessed=6000000, transcendentals=1100000
        ),
    )(dest_slot, lengths, block_mask, tokens, queries, key_weight, value_weight)


def solution(mesh):
    placed = (
        P(("dp", "ctx"), None),
        P(("dp", "ctx"), None),
        P(),
        P(),
        P("dp"),
        P("dp"),
        P("dp", None),
    )
    return jax.shard_map(
        fused if mesh.shape["ctx"] == 4 else on_device,
        mesh=mesh, in_specs=placed, out_specs=P(("dp", "ctx"), None), check_vma=False
    )
```

```python
import jax
import jax.numpy as jnp
from jax import lax
from jax.experimental import pallas as pl
from jax.experimental.pallas import tpu as pltpu
from jax.sharding import PartitionSpec as P

HEADS = 8
HD = 128
BLOCKS_DEV = 4


def clip_index(position, lengths):
    order = jnp.arange(lengths.shape[0], dtype=jnp.int32)
    bounds = jnp.sum(jnp.where(order[None, :] <= order[:, None], lengths[None, :], 0), axis=1)
    return jnp.sum((position[:, None] >= bounds[None, :]).astype(jnp.int32), axis=1)


def collect_rows(wanted, carry, pieces):
    count = pieces[0].shape[0]
    inside = (wanted >= 0) & (wanted < count)
    position = jnp.clip(wanted, 0, count - 1)
    return tuple(
        (
            jnp.where(inside[:, None], jnp.take(piece, position, axis=0), kept)
            for piece, kept in zip(pieces, carry)
        )
    )


def on_device(tokens, queries, key_weight, value_weight, lengths, dest_slot, block_mask):
    device_id = lax.axis_index("ctx")
    row_count = tokens.shape[0]
    inner_width = queries.shape[1]
    block_rows = row_count // BLOCKS_DEV
    block_count = dest_slot.shape[0]
    block_ids = jnp.arange(block_count, dtype=jnp.int32)
    source_block = jnp.zeros((block_count,), jnp.int32).at[dest_slot].set(block_ids)
    my_slots = device_id * BLOCKS_DEV + jnp.arange(BLOCKS_DEV, dtype=jnp.int32)
    mine = source_block[my_slots]
    offsets = jnp.arange(block_rows, dtype=jnp.int32)
    wanted = (mine[:, None] * block_rows + offsets[None, :]).reshape(row_count)
    start_rows = (jnp.zeros_like(tokens), jnp.zeros_like(queries))
    moved_tokens, moved_queries = collect_rows(
        wanted,
        start_rows,
        (
            lax.all_gather(tokens, "ctx", axis=0, tiled=True),
            lax.all_gather(queries, "ctx", axis=0, tiled=True),
        ),
    )
    key_rows = jnp.dot(moved_tokens, key_weight, preferred_element_type=jnp.float32).astype(
        jnp.bfloat16
    )
    value_rows = jnp.dot(moved_tokens, value_weight, preferred_element_type=jnp.float32).astype(
        jnp.bfloat16
    )
    query_clip = clip_index(wanted, lengths)
    query_block_id = wanted // block_rows
    onehot_query = (query_block_id[:, None] == block_ids[None, :]).astype(jnp.float32)
    mask_rows = jnp.dot(onehot_query, block_mask.astype(jnp.float32))
    query_three = moved_queries.reshape(row_count, HEADS, HD)
    score_scale = 1.0 / HD**0.5
    key_piece = lax.all_gather(key_rows, "ctx", axis=0, tiled=True)
    value_piece = lax.all_gather(value_rows, "ctx", axis=0, tiled=True)
    count = key_piece.shape[0]
    key_slot = jnp.arange(count, dtype=jnp.int32)
    key_block = source_block[key_slot // block_rows]
    key_pos = key_block * block_rows + key_slot % block_rows
    key_clip = clip_index(key_pos, lengths)
    onehot_key = (block_ids[:, None] == key_block[None, :]).astype(jnp.float32)
    linked = jnp.dot(mask_rows, onehot_key) > 0.5
    allowed = (query_clip[:, None] == key_clip[None, :]) & (
        (query_block_id[:, None] == key_block[None, :]) | linked
    )
    scores = (
        jnp.einsum(
            "qhd,khd->hqk",
            query_three,
            key_piece.reshape(count, HEADS, HD),
            preferred_element_type=jnp.float32,
        )
        * score_scale
    )
    run_max = jnp.full((HEADS, row_count), -1e30, jnp.float32)
    run_acc = jnp.zeros((row_count, HEADS, HD), jnp.float32)
    masked = jnp.where(allowed[None], scores, jnp.float32(-1e30))
    new_max = jnp.maximum(run_max, jnp.max(masked, axis=-1))
    rescale = jnp.exp(run_max - new_max)
    weights_exp = jnp.where(allowed[None], jnp.exp(masked - new_max[..., None]), jnp.float32(0.0))
    new_total = jnp.sum(weights_exp, axis=-1)
    partial_value = jnp.einsum(
        "hqk,khd->qhd",
        weights_exp.astype(jnp.bfloat16),
        value_piece.reshape(count, HEADS, HD),
        preferred_element_type=jnp.float32,
    )
    new_acc = run_acc * rescale.T[:, :, None] + partial_value
    finished = (
        (new_acc / new_total.T[:, :, None]).reshape(row_count, inner_width).astype(jnp.bfloat16)
    )
    return finished


TOK_CHUNKS = 4
Q_CHUNKS = 2
LOG2E = 1.4426950408889634


def fused_kernel(
    dest,
    lengths,
    mask_ref,
    tok_hbm,
    q_hbm,
    kw_hbm,
    vw_hbm,
    out_ref,
    tok,
    q_own,
    q_send,
    q_all,
    kw,
    vw,
    keys,
    values,
    linked,
    result,
    load_sem,
    tok_send,
    tok_recv,
    relay_send,
    relay_recv,
    near_send,
    near_recv,
    q_ssem,
    q_rsem,
):
    rows, width = tok_hbm.shape
    block_rows = rows // BLOCKS_DEV
    seq = 4 * rows
    blocks = 4 * BLOCKS_DEV
    heads = width // HD
    me = lax.axis_index("ctx")
    near = me + 1 - 2 * (me % 2)
    far = me + 2 - 4 * (me // 2)
    cross = 3 - me
    peers = (me, near, far, cross)

    loads = [
        pltpu.make_async_copy(tok_hbm, tok.at[0], load_sem.at[0]),
        pltpu.make_async_copy(q_hbm, q_own, load_sem.at[1]),
        pltpu.make_async_copy(kw_hbm, kw, load_sem.at[2]),
        pltpu.make_async_copy(vw_hbm, vw, load_sem.at[3]),
    ]
    for load in loads:
        load.start()

    barrier = pltpu.get_barrier_semaphore()
    for peer in peers[1:]:
        pl.semaphore_signal(
            barrier, inc=1, device_id={"ctx": peer}, device_id_type=pl.DeviceIdType.MESH
        )
    pl.semaphore_wait(barrier, 3)

    def send(source, target, send_sem, recv_sem, peer):
        return pltpu.make_async_remote_copy(
            src_ref=source,
            dst_ref=target,
            send_sem=send_sem,
            recv_sem=recv_sem,
            device_id={"ctx": peer},
            device_id_type=pl.DeviceIdType.MESH,
        )

    step = rows // TOK_CHUNKS
    far_copies = []
    relay_copies = []
    for c in range(TOK_CHUNKS):
        part = pl.ds(c * step, step)
        far_copies.append(
            send(tok_hbm.at[part], tok.at[2, part], tok_send.at[c], tok_recv.at[c], far)
        )
        relay_copies.append(
            send(tok.at[2, part], tok.at[3, part], relay_send.at[c], relay_recv.at[c], near)
        )
        far_copies[c].start()
    near_copy = send(tok_hbm, tok.at[1], near_send.at[0], near_recv.at[0], near)
    near_copy.start()

    def two_blocks(source, to):
        count = jnp.int32(0)
        first = jnp.int32(0)
        second = jnp.int32(0)
        for b in range(BLOCKS_DEV):
            hit = dest[source * BLOCKS_DEV + b] // BLOCKS_DEV == to
            first = jnp.where(hit & (count == 0), b, first)
            second = jnp.where(hit & (count == 1), b, second)
            count = count + hit.astype(jnp.int32)
        return first, second

    loads[1].wait()
    qw = width // Q_CHUNKS
    q_copies = {}
    pair = 2 * block_rows

    def pick(shape, pieces, wanted):
        row = lax.broadcasted_iota(jnp.int32, (block_rows, shape), 0)
        column = lax.broadcasted_iota(jnp.int32, (block_rows, shape), 1)
        return jnp.concatenate(
            [jnp.where(row + wanted[p] * block_rows == column, 1.0, 0.0) for p in range(pieces)],
            axis=0,
        ).astype(jnp.bfloat16)

    wanted = []
    for r in range(4):
        wanted.extend(two_blocks(me, peers[r]))
    chosen = pick(rows, 8, wanted)
    for c in range(Q_CHUNKS):
        packed = jnp.dot(
            chosen, q_own[:, c * qw : (c + 1) * qw], preferred_element_type=jnp.float32
        ).astype(jnp.bfloat16)
        q_all[c, 0] = packed[:pair]
        q_send[c] = packed[pair:].reshape(3, pair, qw)
        for r in (1, 3, 2):
            q_copies[c, r] = send(
                q_send.at[c, r - 1],
                q_all.at[c, r],
                q_ssem.at[c, r - 1],
                q_rsem.at[c, r - 1],
                peers[r],
            )
            q_copies[c, r].start()

    bounds = []
    running = jnp.int32(0)
    for c in range(lengths.shape[0]):
        running = running + lengths[c]
        bounds.append(running)

    def clip_of(position):
        total = jnp.zeros_like(position)
        for bound in bounds:
            total = total + jnp.where(position >= bound, 1, 0)
        return total

    col = lax.broadcasted_iota(jnp.int32, (1, seq), 1)
    slot = col // rows
    owner = jnp.where(
        slot == 0, me, jnp.where(slot == 1, near, jnp.where(slot == 2, far, cross))
    )
    key_pos = owner * rows + col % rows
    key_clip = clip_of(key_pos)
    key_block = key_pos // block_rows
    bi = lax.broadcasted_iota(jnp.int32, (blocks, blocks), 0)
    bj = lax.broadcasted_iota(jnp.int32, (blocks, blocks), 1)
    link = jnp.where((bi == bj) | (mask_ref[...] == 1), 1.0, 0.0).astype(jnp.bfloat16)
    spread = jnp.where(
        lax.broadcasted_iota(jnp.int32, (blocks, seq), 0) == key_block, 1.0, 0.0
    ).astype(jnp.bfloat16)
    linked[...] = jnp.dot(link, spread, preferred_element_type=jnp.float32).astype(jnp.bfloat16)

    def blocked_for(first):
        of_block = []
        clips = []
        for r in (first, first + 1):
            for place in two_blocks(peers[r], me):
                block = peers[r] * BLOCKS_DEV + place
                ids = lax.broadcasted_iota(jnp.int32, (block_rows, blocks), 1)
                of_block.append(jnp.where(ids == block, 1.0, 0.0))
                clips.append(
                    clip_of(
                        block * block_rows
                        + lax.broadcasted_iota(jnp.int32, (block_rows, 1), 0)
                    )
                )
        seen = jnp.dot(
            jnp.concatenate(of_block, axis=0).astype(jnp.bfloat16),
            linked[...],
            preferred_element_type=jnp.float32,
        )
        return (seen < 0.5) | (jnp.concatenate(clips, axis=0) != key_clip)

    def project(first, part, parts):
        cw = width // parts
        x = tok[first : first + 2].reshape(2 * rows, width)
        at = slice(first * rows, (first + 2) * rows)
        cols = slice(part * cw, (part + 1) * cw)
        for w, kept in ((kw, keys), (vw, values)):
            kept[at, cols] = jnp.dot(
                x, w[:, cols], preferred_element_type=jnp.float32
            ).astype(jnp.bfloat16)

    def attend(first, blocked, chunk):
        for h in range(heads // Q_CHUNKS):
            q = q_all[chunk, first : first + 2, :, h * HD : (h + 1) * HD].reshape(
                4 * block_rows, HD
            )
            at = chunk * qw + h * HD
            s = lax.dot_general(
                q, keys[:, at : at + HD], (((1,), (1,)), ((), ())),
                preferred_element_type=jnp.float32,
            )
            s = jnp.where(blocked, -jnp.inf, s)
            top = jnp.max(s, axis=1, keepdims=True)
            e = jnp.exp2((s - top) * (LOG2E / HD**0.5))
            total = jnp.sum(e, axis=1, keepdims=True)
            mixed = jnp.dot(
                e.astype(jnp.bfloat16), values[:, at : at + HD],
                preferred_element_type=jnp.float32,
            )
            result[first * 2 * block_rows : (first + 2) * 2 * block_rows, at : at + HD] = (
                mixed / total
            ).astype(jnp.bfloat16)

    near_blocked = blocked_for(0)
    far_blocked = blocked_for(2)

    loads[0].wait()
    loads[2].wait()
    loads[3].wait()
    near_copy.wait_recv()
    for c in range(TOK_CHUNKS):
        project(0, c, TOK_CHUNKS)
        far_copies[c].wait_recv()
        relay_copies[c].start()
    for c in range(TOK_CHUNKS):
        relay_copies[c].wait_recv()
    for c in range(TOK_CHUNKS):
        project(2, c, TOK_CHUNKS)
    wanted = []
    for t in range(BLOCKS_DEV):
        place = jnp.int32(0)
        for r in range(4):
            rank = jnp.int32(0)
            for b in range(BLOCKS_DEV):
                target = dest[peers[r] * BLOCKS_DEV + b]
                hit = target == me * BLOCKS_DEV + t
                place = jnp.where(hit, 2 * r + rank, place)
                rank = rank + (target // BLOCKS_DEV == me).astype(jnp.int32)
        wanted.append(place)
    chosen = pick(2 * rows, BLOCKS_DEV, wanted)
    for c in range(Q_CHUNKS):
        q_copies[c, 1].wait_recv()
        attend(0, near_blocked, c)
    for c in range(Q_CHUNKS):
        q_copies[c, 2].wait_recv()
        q_copies[c, 3].wait_recv()
        attend(2, far_blocked, c)
        out_ref[:, c * qw : (c + 1) * qw] = jnp.dot(
            chosen, result[:, c * qw : (c + 1) * qw], preferred_element_type=jnp.float32
        ).astype(jnp.bfloat16)

    near_copy.wait_send()
    for c in range(TOK_CHUNKS):
        far_copies[c].wait_send()
        relay_copies[c].wait_send()
    for c in q_copies.values():
        c.wait_send()


def fused(tokens, queries, key_weight, value_weight, lengths, dest_slot, block_mask):
    rows, width = tokens.shape
    seq = 4 * rows
    pair = rows // 2
    bf = jnp.bfloat16
    dma = pltpu.SemaphoreType.DMA
    qw = width // Q_CHUNKS
    smem = pl.BlockSpec(memory_space=pltpu.SMEM)
    vmem = pl.BlockSpec(memory_space=pltpu.VMEM)
    hbm = pl.BlockSpec(memory_space=pl.ANY)
    return pl.pallas_call(
        fused_kernel,
        out_shape=pltpu.VMEM((rows, width), bf),
        in_specs=[smem, smem, vmem, hbm, hbm, hbm, hbm],
        out_specs=vmem,
        scratch_shapes=[
            pltpu.VMEM((4, rows, width), bf),
            pltpu.VMEM((rows, width), bf),
            pltpu.VMEM((Q_CHUNKS, 3, pair, qw), bf),
            pltpu.VMEM((Q_CHUNKS, 4, pair, qw), bf),
            pltpu.VMEM(key_weight.shape, bf),
            pltpu.VMEM(value_weight.shape, bf),
            pltpu.VMEM((seq, width), bf),
            pltpu.VMEM((seq, width), bf),
            pltpu.VMEM((4 * BLOCKS_DEV, seq), bf),
            pltpu.VMEM((2 * rows, width), bf),
            dma((4,)),
            dma((TOK_CHUNKS,)),
            dma((TOK_CHUNKS,)),
            dma((TOK_CHUNKS,)),
            dma((TOK_CHUNKS,)),
            dma((1,)),
            dma((1,)),
            dma((Q_CHUNKS, 3)),
            dma((Q_CHUNKS, 3)),
        ],
        compiler_params=pltpu.CompilerParams(
            collective_id=0, has_side_effects=True, vmem_limit_bytes=58 * 2**20
        ),
        cost_estimate=pl.CostEstimate(
            flops=2800000000, bytes_accessed=6000000, transcendentals=1100000
        ),
    )(dest_slot, lengths, block_mask, tokens, queries, key_weight, value_weight)


def solution(mesh):
    placed = (
        P(("dp", "ctx"), None),
        P(("dp", "ctx"), None),
        P(),
        P(),
        P("dp"),
        P("dp"),
        P("dp", None),
    )
    return jax.shard_map(
        fused if mesh.shape["ctx"] == 4 else on_device,
        mesh=mesh, in_specs=placed, out_specs=P(("dp", "ctx"), None), check_vma=False
    )
```

```python
import jax
import jax.numpy as jnp
from jax import lax
from jax.experimental import pallas as pl
from jax.experimental.pallas import tpu as pltpu
from jax.sharding import PartitionSpec as P

HEADS = 8
HD = 128
BLOCKS_DEV = 4


def clip_index(position, lengths):
    order = jnp.arange(lengths.shape[0], dtype=jnp.int32)
    bounds = jnp.sum(jnp.where(order[None, :] <= order[:, None], lengths[None, :], 0), axis=1)
    return jnp.sum((position[:, None] >= bounds[None, :]).astype(jnp.int32), axis=1)


def collect_rows(wanted, carry, pieces):
    count = pieces[0].shape[0]
    inside = (wanted >= 0) & (wanted < count)
    position = jnp.clip(wanted, 0, count - 1)
    return tuple(
        (
            jnp.where(inside[:, None], jnp.take(piece, position, axis=0), kept)
            for piece, kept in zip(pieces, carry)
        )
    )


def on_device(tokens, queries, key_weight, value_weight, lengths, dest_slot, block_mask):
    device_id = lax.axis_index("ctx")
    row_count = tokens.shape[0]
    inner_width = queries.shape[1]
    block_rows = row_count // BLOCKS_DEV
    block_count = dest_slot.shape[0]
    block_ids = jnp.arange(block_count, dtype=jnp.int32)
    source_block = jnp.zeros((block_count,), jnp.int32).at[dest_slot].set(block_ids)
    my_slots = device_id * BLOCKS_DEV + jnp.arange(BLOCKS_DEV, dtype=jnp.int32)
    mine = source_block[my_slots]
    offsets = jnp.arange(block_rows, dtype=jnp.int32)
    wanted = (mine[:, None] * block_rows + offsets[None, :]).reshape(row_count)
    start_rows = (jnp.zeros_like(tokens), jnp.zeros_like(queries))
    moved_tokens, moved_queries = collect_rows(
        wanted,
        start_rows,
        (
            lax.all_gather(tokens, "ctx", axis=0, tiled=True),
            lax.all_gather(queries, "ctx", axis=0, tiled=True),
        ),
    )
    key_rows = jnp.dot(moved_tokens, key_weight, preferred_element_type=jnp.float32).astype(
        jnp.bfloat16
    )
    value_rows = jnp.dot(moved_tokens, value_weight, preferred_element_type=jnp.float32).astype(
        jnp.bfloat16
    )
    query_clip = clip_index(wanted, lengths)
    query_block_id = wanted // block_rows
    onehot_query = (query_block_id[:, None] == block_ids[None, :]).astype(jnp.float32)
    mask_rows = jnp.dot(onehot_query, block_mask.astype(jnp.float32))
    query_three = moved_queries.reshape(row_count, HEADS, HD)
    score_scale = 1.0 / HD**0.5
    key_piece = lax.all_gather(key_rows, "ctx", axis=0, tiled=True)
    value_piece = lax.all_gather(value_rows, "ctx", axis=0, tiled=True)
    count = key_piece.shape[0]
    key_slot = jnp.arange(count, dtype=jnp.int32)
    key_block = source_block[key_slot // block_rows]
    key_pos = key_block * block_rows + key_slot % block_rows
    key_clip = clip_index(key_pos, lengths)
    onehot_key = (block_ids[:, None] == key_block[None, :]).astype(jnp.float32)
    linked = jnp.dot(mask_rows, onehot_key) > 0.5
    allowed = (query_clip[:, None] == key_clip[None, :]) & (
        (query_block_id[:, None] == key_block[None, :]) | linked
    )
    scores = (
        jnp.einsum(
            "qhd,khd->hqk",
            query_three,
            key_piece.reshape(count, HEADS, HD),
            preferred_element_type=jnp.float32,
        )
        * score_scale
    )
    run_max = jnp.full((HEADS, row_count), -1e30, jnp.float32)
    run_acc = jnp.zeros((row_count, HEADS, HD), jnp.float32)
    masked = jnp.where(allowed[None], scores, jnp.float32(-1e30))
    new_max = jnp.maximum(run_max, jnp.max(masked, axis=-1))
    rescale = jnp.exp(run_max - new_max)
    weights_exp = jnp.where(allowed[None], jnp.exp(masked - new_max[..., None]), jnp.float32(0.0))
    new_total = jnp.sum(weights_exp, axis=-1)
    partial_value = jnp.einsum(
        "hqk,khd->qhd",
        weights_exp.astype(jnp.bfloat16),
        value_piece.reshape(count, HEADS, HD),
        preferred_element_type=jnp.float32,
    )
    new_acc = run_acc * rescale.T[:, :, None] + partial_value
    finished = (
        (new_acc / new_total.T[:, :, None]).reshape(row_count, inner_width).astype(jnp.bfloat16)
    )
    return finished


TOK_CHUNKS = 4
Q_CHUNKS = 2
Q_EARLY = 0
Q_AFTER = {1: (0,), 3: (1,)}
LOG2E = 1.4426950408889634


def fused_kernel(
    dest,
    lengths,
    mask_ref,
    tok_hbm,
    q_hbm,
    kw_hbm,
    vw_hbm,
    out_ref,
    tok,
    q_own,
    q_send,
    q_all,
    kw,
    vw,
    keys,
    values,
    linked,
    bias,
    result,
    load_sem,
    tok_send,
    tok_recv,
    relay_send,
    relay_recv,
    near_send,
    near_recv,
    q_ssem,
    q_rsem,
):
    rows, width = tok_hbm.shape
    block_rows = rows // BLOCKS_DEV
    seq = 4 * rows
    blocks = 4 * BLOCKS_DEV
    heads = width // HD
    me = lax.axis_index("ctx")
    near = me + 1 - 2 * (me % 2)
    far = me + 2 - 4 * (me // 2)
    cross = 3 - me
    peers = (me, near, far, cross)

    loads = [
        pltpu.make_async_copy(tok_hbm, tok.at[0], load_sem.at[0]),
        pltpu.make_async_copy(q_hbm, q_own, load_sem.at[1]),
        pltpu.make_async_copy(kw_hbm, kw, load_sem.at[2]),
        pltpu.make_async_copy(vw_hbm, vw, load_sem.at[3]),
    ]
    for load in loads:
        load.start()

    barrier = pltpu.get_barrier_semaphore()
    for peer in peers[1:]:
        pl.semaphore_signal(
            barrier, inc=1, device_id={"ctx": peer}, device_id_type=pl.DeviceIdType.MESH
        )
    pl.semaphore_wait(barrier, 3)

    def send(source, target, send_sem, recv_sem, peer):
        return pltpu.make_async_remote_copy(
            src_ref=source,
            dst_ref=target,
            send_sem=send_sem,
            recv_sem=recv_sem,
            device_id={"ctx": peer},
            device_id_type=pl.DeviceIdType.MESH,
        )

    step = rows // TOK_CHUNKS
    far_copies = []
    relay_copies = []
    for c in range(TOK_CHUNKS):
        part = pl.ds(c * step, step)
        far_copies.append(
            send(tok_hbm.at[part], tok.at[2, part], tok_send.at[c], tok_recv.at[c], far)
        )
        relay_copies.append(
            send(tok.at[2, part], tok.at[3, part], relay_send.at[c], relay_recv.at[c], near)
        )
        far_copies[c].start()
    near_copy = send(tok_hbm, tok.at[1], near_send.at[0], near_recv.at[0], near)
    near_copy.start()

    def two_blocks(source, to):
        count = jnp.int32(0)
        first = jnp.int32(0)
        second = jnp.int32(0)
        for b in range(BLOCKS_DEV):
            hit = dest[source * BLOCKS_DEV + b] // BLOCKS_DEV == to
            first = jnp.where(hit & (count == 0), b, first)
            second = jnp.where(hit & (count == 1), b, second)
            count = count + hit.astype(jnp.int32)
        return first, second

    loads[1].wait()
    qw = width // Q_CHUNKS
    q_copies = {}
    pair = 2 * block_rows

    def pick(shape, pieces, wanted):
        row = lax.broadcasted_iota(jnp.int32, (block_rows, shape), 0)
        column = lax.broadcasted_iota(jnp.int32, (block_rows, shape), 1)
        return jnp.concatenate(
            [jnp.where(row + wanted[p] * block_rows == column, 1.0, 0.0) for p in range(pieces)],
            axis=0,
        ).astype(jnp.bfloat16)

    wanted = []
    for r in range(4):
        wanted.extend(two_blocks(me, peers[r]))
    chosen = pick(rows, 8, wanted)
    for c in range(Q_CHUNKS):
        packed = jnp.dot(
            chosen, q_own[:, c * qw : (c + 1) * qw], preferred_element_type=jnp.float32
        ).astype(jnp.bfloat16)
        q_all[c, 0] = packed[:pair]
        q_send[c] = packed[pair:].reshape(3, pair, qw)
        for r in (1, 3, 2):
            q_copies[c, r] = send(
                q_send.at[c, r - 1],
                q_all.at[c, r],
                q_ssem.at[c, r - 1],
                q_rsem.at[c, r - 1],
                peers[r],
            )
            if r == 1 or c < Q_EARLY:
                q_copies[c, r].start()

    bounds = []
    running = jnp.int32(0)
    for c in range(lengths.shape[0]):
        running = running + lengths[c]
        bounds.append(running)

    def clip_of(position):
        total = jnp.zeros_like(position)
        for bound in bounds:
            total = total + jnp.where(position >= bound, 1, 0)
        return total

    col = lax.broadcasted_iota(jnp.int32, (1, seq), 1)
    slot = col // rows
    owner = jnp.where(
        slot == 0, me, jnp.where(slot == 1, near, jnp.where(slot == 2, far, cross))
    )
    key_pos = owner * rows + col % rows
    key_clip = clip_of(key_pos)
    key_block = key_pos // block_rows
    bi = lax.broadcasted_iota(jnp.int32, (blocks, blocks), 0)
    bj = lax.broadcasted_iota(jnp.int32, (blocks, blocks), 1)
    link = jnp.where((bi == bj) | (mask_ref[...] == 1), 1.0, 0.0).astype(jnp.bfloat16)
    spread = jnp.where(
        lax.broadcasted_iota(jnp.int32, (blocks, seq), 0) == key_block, 1.0, 0.0
    ).astype(jnp.bfloat16)
    linked[...] = jnp.dot(link, spread, preferred_element_type=jnp.float32).astype(jnp.bfloat16)

    def blocked_for(first):
        of_block = []
        clips = []
        for r in (first, first + 1):
            for place in two_blocks(peers[r], me):
                block = peers[r] * BLOCKS_DEV + place
                ids = lax.broadcasted_iota(jnp.int32, (block_rows, blocks), 1)
                of_block.append(jnp.where(ids == block, 1.0, 0.0))
                clips.append(
                    clip_of(
                        block * block_rows
                        + lax.broadcasted_iota(jnp.int32, (block_rows, 1), 0)
                    )
                )
        seen = jnp.dot(
            jnp.concatenate(of_block, axis=0).astype(jnp.bfloat16),
            linked[...],
            preferred_element_type=jnp.float32,
        )
        return (seen < 0.5) | (jnp.concatenate(clips, axis=0) != key_clip)

    def project(first, part, parts, count=2):
        cw = width // parts
        x = tok[first : first + count].reshape(count * rows, width)
        at = slice(first * rows, (first + count) * rows)
        cols = slice(part * cw, (part + 1) * cw)
        for w, kept in ((kw, keys), (vw, values)):
            kept[at, cols] = jnp.dot(
                x, w[:, cols], preferred_element_type=jnp.float32
            ).astype(jnp.bfloat16)

    def attend(first, chunk):
        for h in range(heads // Q_CHUNKS):
            q = q_all[chunk, first : first + 2, :, h * HD : (h + 1) * HD].reshape(
                4 * block_rows, HD
            )
            at = chunk * qw + h * HD
            s = lax.dot_general(
                q, keys[:, at : at + HD], (((1,), (1,)), ((), ())),
                preferred_element_type=jnp.float32,
            )
            s = s + bias[first // 2]
            top = jnp.max(s, axis=1, keepdims=True)
            e = jnp.exp2((s - top) * (LOG2E / HD**0.5))
            total = jnp.sum(e, axis=1, keepdims=True)
            mixed = jnp.dot(
                e.astype(jnp.bfloat16), values[:, at : at + HD],
                preferred_element_type=jnp.float32,
            )
            result[first * 2 * block_rows : (first + 2) * 2 * block_rows, at : at + HD] = (
                mixed / total
            ).astype(jnp.bfloat16)

    bias[0] = jnp.where(blocked_for(0), -jnp.inf, 0.0)
    bias[1] = jnp.where(blocked_for(2), -jnp.inf, 0.0)

    loads[0].wait()
    loads[2].wait()
    loads[3].wait()
    near_copy.wait_recv()
    for c in range(TOK_CHUNKS):
        project(0, c, TOK_CHUNKS)
        far_copies[c].wait_recv()
        relay_copies[c].start()
        for later in Q_AFTER.get(c, ()):
            q_copies[later, 3].start()
            q_copies[later, 2].start()
    for c in range(TOK_CHUNKS):
        project(2, c, TOK_CHUNKS, 1)
    for c in range(TOK_CHUNKS):
        relay_copies[c].wait_recv()
    for c in range(TOK_CHUNKS):
        project(3, c, TOK_CHUNKS, 1)
    wanted = []
    for t in range(BLOCKS_DEV):
        place = jnp.int32(0)
        for r in range(4):
            rank = jnp.int32(0)
            for b in range(BLOCKS_DEV):
                target = dest[peers[r] * BLOCKS_DEV + b]
                hit = target == me * BLOCKS_DEV + t
                place = jnp.where(hit, 2 * r + rank, place)
                rank = rank + (target // BLOCKS_DEV == me).astype(jnp.int32)
        wanted.append(place)
    chosen = pick(2 * rows, BLOCKS_DEV, wanted)
    for c in range(Q_CHUNKS):
        q_copies[c, 1].wait_recv()
        attend(0, c)
    for c in range(Q_CHUNKS):
        q_copies[c, 2].wait_recv()
        q_copies[c, 3].wait_recv()
        attend(2, c)
        out_ref[:, c * qw : (c + 1) * qw] = jnp.dot(
            chosen, result[:, c * qw : (c + 1) * qw], preferred_element_type=jnp.float32
        ).astype(jnp.bfloat16)

    near_copy.wait_send()
    for c in range(TOK_CHUNKS):
        far_copies[c].wait_send()
        relay_copies[c].wait_send()
    for c in q_copies.values():
        c.wait_send()


def fused(tokens, queries, key_weight, value_weight, lengths, dest_slot, block_mask):
    rows, width = tokens.shape
    seq = 4 * rows
    pair = rows // 2
    bf = jnp.bfloat16
    dma = pltpu.SemaphoreType.DMA
    qw = width // Q_CHUNKS
    smem = pl.BlockSpec(memory_space=pltpu.SMEM)
    vmem = pl.BlockSpec(memory_space=pltpu.VMEM)
    hbm = pl.BlockSpec(memory_space=pl.ANY)
    return pl.pallas_call(
        fused_kernel,
        out_shape=pltpu.VMEM((rows, width), bf),
        in_specs=[smem, smem, vmem, hbm, hbm, hbm, hbm],
        out_specs=vmem,
        scratch_shapes=[
            pltpu.VMEM((4, rows, width), bf),
            pltpu.VMEM((rows, width), bf),
            pltpu.VMEM((Q_CHUNKS, 3, pair, qw), bf),
            pltpu.VMEM((Q_CHUNKS, 4, pair, qw), bf),
            pltpu.VMEM(key_weight.shape, bf),
            pltpu.VMEM(value_weight.shape, bf),
            pltpu.VMEM((seq, width), bf),
            pltpu.VMEM((seq, width), bf),
            pltpu.VMEM((4 * BLOCKS_DEV, seq), bf),
            pltpu.VMEM((2, rows, seq), jnp.float32),
            pltpu.VMEM((2 * rows, width), bf),
            dma((4,)),
            dma((TOK_CHUNKS,)),
            dma((TOK_CHUNKS,)),
            dma((TOK_CHUNKS,)),
            dma((TOK_CHUNKS,)),
            dma((1,)),
            dma((1,)),
            dma((Q_CHUNKS, 3)),
            dma((Q_CHUNKS, 3)),
        ],
        compiler_params=pltpu.CompilerParams(
            collective_id=0, has_side_effects=True, vmem_limit_bytes=58 * 2**20
        ),
        cost_estimate=pl.CostEstimate(
            flops=2800000000, bytes_accessed=6000000, transcendentals=1100000
        ),
    )(dest_slot, lengths, block_mask, tokens, queries, key_weight, value_weight)


def solution(mesh):
    placed = (
        P(("dp", "ctx"), None),
        P(("dp", "ctx"), None),
        P(),
        P(),
        P("dp"),
        P("dp"),
        P("dp", None),
    )
    return jax.shard_map(
        fused if mesh.shape["ctx"] == 4 else on_device,
        mesh=mesh, in_specs=placed, out_specs=P(("dp", "ctx"), None), check_vma=False
    )
```
